512 devices in a mesh: req: 32 (over y, x), seq: 16 (over z, core).
Axes of the slice: x: 4, y: 8, z: 8, core: 2. Of those that a mesh axis runs over, the one named last changes fastest.
Arguments:
- queries: bfloat16 [65536, 4096], P(('req', 'seq')), parts along dimension 0, may hold values from -6 to 6
- span_keys: bfloat16 [65536, 512], P(('req', 'seq')), parts along dimension 0, may hold values from -6 to 6
- span_values: bfloat16 [65536, 512], P(('req', 'seq')), parts along dimension 0, may hold values from -6 to 6
- cache_keys: bfloat16 [65536, 512], P(('req', 'seq')), parts along dimension 0, may hold values from -6 to 6
- cache_values: bfloat16 [65536, 512], P(('req', 'seq')), parts along dimension 0, may hold values from -6 to 6
- block_lists: int32 [512, 32, 4], P(('req', 'seq')), parts along dimension 0, may hold values from 0 to 31, as said below
Outputs:
- attended: bfloat16 [65536, 4096], P(('req', 'seq')), parts along dimension 0
The draws below stay inside these ranges and needn't reach their ends.
There are 32 independent parts, one for each index of `req`. The reference program is written for one: setup_inputs(seed, part) draws one part's arguments, and reference() takes and returns one part's arrays. A program takes and returns all parts, laid end to end along the dimension named above; each array names one. Nothing has to cross between parts.
Inputs may be any that keep to these rules, and one draw needn't show every extreme that they name: block_lists[i, h] holds 4 different key block indices, none above 16 + i; it always holds block 0 and the blocks 16 + i - 1 to 16 + i.
All inputs are finite; a program needn't handle non-finite values.
Results may differ from the reference program's by a relative error of at most 0.0049.
Values may be sent and summed in bfloat16 or wider, within the bound.
No kernel may reach another device: no remote copies, remote signals or barrier semaphores. Data moves between devices by JAX's collectives and lax.ppermute only.
A program may use at most 64 MiB of HBM per device.

```python
import math
import jax
import jax.numpy as jnp
from jax import lax

QUERY_HEADS_HALF = 32
KVH = 4
DH = 128
BLK = 128
NSEL = 4
LOCAL = 2
SPAN = 2048
CACHE = 2048
QBLOCKS = 16
CBLOCKS = 16


def draw_queries(key, part):
    key = jax.random.fold_in(key, 11)
    entries = jax.random.truncated_normal(key, -6.0, 6.0, (SPAN, QUERY_HEADS_HALF, DH), jnp.float32)
    return entries.reshape(SPAN, QUERY_HEADS_HALF * DH).astype(jnp.bfloat16)


def draw_cache_keys(key, part):
    key = jax.random.fold_in(key, 23)
    entries = jax.random.truncated_normal(key, -6.0, 6.0, (CACHE, KVH, DH), jnp.float32)
    return entries.reshape(CACHE, KVH * DH).astype(jnp.bfloat16)


def draw_block_lists(key, part):
    key = jax.random.fold_in(key, 37)
    noise_key, column_key, slash_key = jax.random.split(key, 3)
    block_total = CBLOCKS + QBLOCKS
    picked_count = NSEL - 1 - LOCAL
    query_index = jnp.arange(QBLOCKS, dtype=jnp.int32)[:, None, None]
    column = jnp.arange(block_total, dtype=jnp.int32)[None, None, :]
    diagonal = CBLOCKS + query_index
    random_rating = jax.random.randint(noise_key, (QBLOCKS, QUERY_HEADS_HALF, block_total), 0, 4096)
    column_blocks_chosen = jax.random.randint(column_key, (QUERY_HEADS_HALF, block_total), 0, 2)
    diagonal_selection = jax.random.randint(slash_key, (QUERY_HEADS_HALF, block_total), 0, 2)
    block_separation = jnp.clip(diagonal - column, 0, block_total - 1)
    diagonal_boost = diagonal_selection[jnp.arange(QUERY_HEADS_HALF)[None, :, None], block_separation]
    key_block_rating = random_rating + 8192 * column_blocks_chosen[None, :, :] + 8192 * diagonal_boost
    allowed = (column >= 1) & (column <= diagonal - LOCAL)
    key_block_rating = jnp.where(allowed, key_block_rating * block_total + column, -1)
    ignored, chosen = lax.top_k(key_block_rating, picked_count)
    fixed_blocks = [jnp.zeros((QBLOCKS, QUERY_HEADS_HALF, 1), jnp.int32)]
    for back in range(LOCAL):
        fixed_blocks.append(jnp.broadcast_to(diagonal - back, (QBLOCKS, QUERY_HEADS_HALF, 1)).astype(jnp.int32))
    return jnp.concatenate(fixed_blocks + [chosen.astype(jnp.int32)], axis=2).astype(jnp.int32)


def steps_of(key, dims, cuts, smallest, top_value):
    gain, own = 1.0, jax.random.fold_in(key, 6)
    for position, blocks in cuts:
        draws = jnp.exp(jax.random.uniform(jax.random.fold_in(own, position), (blocks,), jnp.float32, smallest / len(cuts), top_value / len(cuts)))
        gain = gain * jnp.repeat(draws, dims[position] // blocks).reshape([-1 if axis == position else 1 for axis in range(len(dims))])
    return gain


def scatter_about(key, shape, spread, most, cuts=(), kind=jnp.bfloat16):
    values = spread * jax.random.normal(key, shape, jnp.float32)
    if cuts:
        values = values * steps_of(key, shape, cuts, -0.22, 0.18)
    return jnp.clip(values, -most, most).astype(kind)


def setup_inputs(seed: int = 0, part: int = 0) -> dict:
    splits = jax.random.split(jax.random.key(seed), 7)
    part_splits = jax.random.split(jax.random.fold_in(splits[6], part), 7)
    queries = draw_queries(jax.random.fold_in(jax.random.fold_in(splits[6], part), 71), part)
    span_keys = scatter_about(part_splits[1], (SPAN, KVH * DH), 1.0, 6.0, ((0, 16),))
    span_values = scatter_about(part_splits[2], (SPAN, KVH * DH), 1.0, 6.0, ((0, 16),))
    cache_keys = draw_cache_keys(jax.random.fold_in(jax.random.fold_in(splits[6], part), 71), part)
    cache_values = scatter_about(part_splits[4], (CACHE, KVH * DH), 1.0, 6.0, ((0, 16),))
    block_lists = draw_block_lists(jax.random.fold_in(jax.random.fold_in(splits[6], part), 71), part)
    return dict(queries=queries, span_keys=span_keys, span_values=span_values, cache_keys=cache_keys, cache_values=cache_values, block_lists=block_lists)


def reference(queries, span_keys, span_values, cache_keys, cache_values, block_lists):
    all_keys = jnp.concatenate([cache_keys, span_keys], axis=0)
    all_values = jnp.concatenate([cache_values, span_values], axis=0)
    block_total = all_keys.shape[0] // BLK
    key_blocks = all_keys.reshape(block_total, BLK, KVH, DH)
    value_blocks = all_values.reshape(block_total, BLK, KVH, DH)
    kv_of_head = (jnp.arange(QUERY_HEADS_HALF, dtype=jnp.int32) // (QUERY_HEADS_HALF // KVH)).astype(jnp.int32)
    query_blocks = queries.reshape(QBLOCKS, BLK, QUERY_HEADS_HALF, DH)
    offsets = (jnp.arange(QBLOCKS, dtype=jnp.int32) * BLK).astype(jnp.int32)
    score_scale = 1.0 / math.sqrt(DH)

    def one_block(member):
        query_block, head_lists, offset = member
        picked_keys = key_blocks[head_lists, :, kv_of_head[:, None]].astype(jnp.float32)
        picked_values = value_blocks[head_lists, :, kv_of_head[:, None]].astype(jnp.float32)
        scores = jnp.einsum('rhd,hscd->hrsc', query_block.astype(jnp.float32), picked_keys) * score_scale
        key_position = head_lists[:, :, None] * BLK + jnp.arange(BLK, dtype=jnp.int32)[None, None, :]
        query_position = CACHE + offset + jnp.arange(BLK, dtype=jnp.int32)
        allowed = key_position[:, None, :, :] <= query_position[None, :, None, None]
        scores = jnp.where(allowed, scores, -jnp.inf)
        row_max = lax.optimization_barrier(jnp.max(scores, axis=(2, 3), keepdims=True))
        powers = jnp.exp(scores - row_max)
        weights = (powers / lax.optimization_barrier(jnp.sum(powers, axis=(2, 3), keepdims=True))).astype(jnp.bfloat16)
        mixed_rows = jnp.einsum('hrsc,hscd->rhd', weights.astype(jnp.float32), picked_values)
        return mixed_rows.astype(jnp.bfloat16)
    result = lax.map(one_block, (query_blocks, block_lists, offsets))
    return result.reshape(SPAN, QUERY_HEADS_HALF * DH)
```

```python
import math

import jax
import jax.numpy as jnp
import numpy as np
from jax import lax
from jax.experimental import pallas as pl
from jax.experimental.pallas import tpu as pltpu
from jax.sharding import PartitionSpec as P

HEADS = 32
KVH = 4
GROUP = HEADS // KVH
DH = 128
BLK = 128
WIDTH = KVH * DH
SEQ = 16
CHIPS = SEQ // 2
SCALE = math.log2(math.e) / math.sqrt(DH)

RING = [(2 * z, 2 * ((z + 1) % CHIPS)) for z in range(CHIPS)] + [
    (2 * z + 1, 2 * ((z - 1) % CHIPS) + 1) for z in range(CHIPS)
]
SWAP = [(i, i ^ 1) for i in range(SEQ)]

NAMES = ["own", "oth"] + [
    kind + str(step) + lane
    for step in (1, 2, 3, 4)
    for lane in ("A", "B")
    for kind in ("got", "swp")
    if (step, lane) != (4, "B")
]


def slot_table():
    table = np.zeros((2, CHIPS, 2), np.int32)
    for core in range(2):
        for away in range(CHIPS):
            for owner in range(2):
                if away == 0:
                    name = "own" if owner == core else "oth"
                else:
                    down = away < 4 or (away == 4 and owner == 1)
                    step = away if down else CHIPS - away
                    lane = "A" if owner == (1 if down else 0) else "B"
                    kind = "got" if core == (1 if down else 0) else "swp"
                    name = kind + str(step) + lane
                table[core, away, owner] = NAMES.index(name)
    return table


def pick(slot, low, high, use):
    if high - low == 1:
        use(low)
        return
    middle = (low + high) // 2

    @pl.when(slot < middle)
    def _():
        pick(slot, low, middle, use)

    @pl.when(slot >= middle)
    def _():
        pick(slot, middle, high, use)


def attend_kernel(slot_ref, half_ref, q_ref, *refs):
    held = refs[: len(NAMES)]
    o_ref, k_fix, v_fix, k_pick, v_pick, fix_sem, pick_sem = refs[len(NAMES) :]

    def fix_copies(n, buffer, half):
        column = pl.multiple_of(half * 2 * WIDTH, 2 * WIDTH)
        return (
            pltpu.make_async_copy(held[buffer].at[:, pl.ds(column, WIDTH)], k_fix.at[n], fix_sem.at[n, 0]),
            pltpu.make_async_copy(held[buffer].at[:, pl.ds(column + WIDTH, WIDTH)], v_fix.at[n], fix_sem.at[n, 1]),
        )

    def pick_copies(h, buffer, half):
        column = pl.multiple_of(half * 2 * WIDTH + (h // GROUP) * DH, DH)
        return (
            pltpu.make_async_copy(held[buffer].at[:, pl.ds(column, DH)], k_pick.at[h], pick_sem.at[h, 0]),
            pltpu.make_async_copy(held[buffer].at[:, pl.ds(column + WIDTH, DH)], v_pick.at[h], pick_sem.at[h, 1]),
        )

    def start(copies):
        for copy in copies:
            copy.start()

    start(fix_copies(2, 0, 1))
    for n in range(2):
        pick(slot_ref[HEADS + n], 0, len(NAMES), lambda b: start(fix_copies(n, b, half_ref[HEADS + n])))

    def start_head(h, carry):
        pick(slot_ref[h], 0, len(NAMES), lambda b: start(pick_copies(h, b, half_ref[h])))
        return carry

    lax.fori_loop(0, HEADS, start_head, 0)

    for n in range(3):
        for copy in fix_copies(n, 0, 0):
            copy.wait()
    row = lax.broadcasted_iota(jnp.int32, (BLK, BLK), 0)
    col = lax.broadcasted_iota(jnp.int32, (BLK, BLK), 1)
    seen = col <= row
    over_rows = (((1,), (1,)), ((), ()))
    over_keys = (((1,), (0,)), ((), ()))
    for g in range(KVH):
        cols = slice(g * DH, (g + 1) * DH)
        keys = jnp.concatenate([k_fix[n, :, cols] for n in range(3)], axis=0)
        values = jnp.concatenate([v_fix[n, :, cols] for n in range(3)], axis=0)
        heads = range(g * GROUP, (g + 1) * GROUP)
        queries = jnp.concatenate([q_ref[:, h * DH : (h + 1) * DH] for h in heads], axis=0)
        fixed = lax.dot_general(queries, keys, over_rows, preferred_element_type=jnp.float32)
        for h in heads:
            for copy in pick_copies(h, 0, 0):
                copy.wait()
        powers_fixed, powers_picked, sums = [], [], []
        for n, h in enumerate(heads):
            part = fixed[n * BLK : (n + 1) * BLK]
            old = part[:, : 2 * BLK]
            new = jnp.where(seen, part[:, 2 * BLK :], -jnp.inf)
            picked = lax.dot_general(
                q_ref[:, h * DH : (h + 1) * DH], k_pick[h], over_rows, preferred_element_type=jnp.float32
            )
            scores = jnp.concatenate([old, new, picked], axis=1)
            top = jnp.max(scores, axis=1, keepdims=True)
            powers = jnp.exp2((scores - top) * SCALE)
            sums.append(jnp.sum(powers, axis=1, keepdims=True))
            powers = powers.astype(jnp.bfloat16)
            powers_fixed.append(powers[:, : 3 * BLK])
            powers_picked.append(powers[:, 3 * BLK :])
        mixed = lax.dot_general(
            jnp.concatenate(powers_fixed, axis=0), values, over_keys, preferred_element_type=jnp.float32
        )
        for n, h in enumerate(heads):
            total = mixed[n * BLK : (n + 1) * BLK] + lax.dot_general(
                powers_picked[n], v_pick[h], over_keys, preferred_element_type=jnp.float32
            )
            o_ref[:, h * DH : (h + 1) * DH] = (total / sums[n]).astype(jnp.bfloat16)


def attend(slots, halves, queries, held):
    return pl.pallas_call(
        attend_kernel,
        out_shape=jax.ShapeDtypeStruct((BLK, HEADS * DH), jnp.bfloat16),
        in_specs=[pl.BlockSpec(memory_space=pltpu.SMEM)] * 2
        + [pl.BlockSpec(memory_space=pltpu.VMEM)]
        + [pl.BlockSpec(memory_space=pl.ANY)] * len(NAMES),
        out_specs=pl.BlockSpec(memory_space=pltpu.VMEM),
        scratch_shapes=[
            pltpu.VMEM((3, BLK, WIDTH), jnp.bfloat16),
            pltpu.VMEM((3, BLK, WIDTH), jnp.bfloat16),
            pltpu.VMEM((HEADS, BLK, DH), jnp.bfloat16),
            pltpu.VMEM((HEADS, BLK, DH), jnp.bfloat16),
            pltpu.SemaphoreType.DMA((3, 2)),
            pltpu.SemaphoreType.DMA((HEADS, 2)),
        ],
        compiler_params=pltpu.CompilerParams(vmem_limit_bytes=32 * 1024 * 1024),
        cost_estimate=pl.CostEstimate(flops=1 << 30, bytes_accessed=6 << 20, transcendentals=1 << 21),
    )(slots, halves, queries, *held)


def shards(queries, span_keys, span_values, cache_keys, cache_values, block_lists):
    me = lax.axis_index("seq")
    own = jnp.concatenate([cache_keys, cache_values, span_keys, span_values], axis=1)
    held = {"own": own, "oth": lax.ppermute(own, "seq", SWAP)}
    last = {"A": held["own"], "B": held["oth"]}
    for step in (1, 2, 3, 4):
        for lane in ("A", "B"):
            if (step, lane) == (4, "B"):
                continue
            last[lane] = lax.ppermute(last[lane], "seq", RING)
            held["got" + str(step) + lane] = last[lane]
            held["swp" + str(step) + lane] = lax.ppermute(last[lane], "seq", SWAP)

    lists = block_lists.reshape(HEADS, 4)
    chosen = jnp.sum(lists, axis=1) - (2 * (SEQ + me) - 1)
    blocks = jnp.concatenate([chosen, jnp.zeros((1,), jnp.int32), (SEQ + me - 1).reshape(1)]).astype(jnp.int32)
    blocks = jnp.clip(blocks, 0, 2 * SEQ - 1)
    owner = blocks % SEQ
    away = (owner // 2 - me // 2) % CHIPS
    table = jnp.asarray(slot_table().reshape(-1))
    slots = table[(me % 2) * 2 * CHIPS + away * 2 + owner % 2]
    return attend(slots, blocks // SEQ, queries, [held[name] for name in NAMES])


def solution(mesh):
    rows = P(("req", "seq"), None)
    return jax.shard_map(
        shards,
        mesh=mesh,
        in_specs=(rows,) * 5 + (P(("req", "seq"), None, None),),
        out_specs=rows,
        check_vma=False,
    )
```

```python
import math

import jax
import jax.numpy as jnp
import numpy as np
from jax import lax
from jax.experimental import pallas as pl
from jax.experimental.pallas import tpu as pltpu
from jax.sharding import PartitionSpec as P

HEADS = 32
KVH = 4
GROUP = HEADS // KVH
DH = 128
BLK = 128
WIDTH = KVH * DH
SEQ = 16
CHIPS = SEQ // 2
SCALE = math.log2(math.e) / math.sqrt(DH)

RING = [(2 * z, 2 * ((z + 1) % CHIPS)) for z in range(CHIPS)] + [
    (2 * z + 1, 2 * ((z - 1) % CHIPS) + 1) for z in range(CHIPS)
]
CROSS = [(2 * z + 1, 2 * ((z + 1) % CHIPS)) for z in range(CHIPS)] + [
    (2 * z, 2 * ((z - 1) % CHIPS) + 1) for z in range(CHIPS)
]
SWAP = [(i, i ^ 1) for i in range(SEQ)]

NAMES = ["own", "oth"] + [
    kind + str(step) + lane
    for step in (1, 2, 3, 4)
    for lane in ("A", "B")
    for kind in ("got", "swp")
    if (step, lane) != (4, "B")
]


def slot_table():
    table = np.zeros((2, CHIPS, 2), np.int32)
    for core in range(2):
        for away in range(CHIPS):
            for owner in range(2):
                if away == 0:
                    name = "own" if owner == core else "oth"
                else:
                    down = away < 4 or (away == 4 and owner == 1)
                    step = away if down else CHIPS - away
                    lane = "A" if owner == (1 if down else 0) else "B"
                    kind = "got" if core == (1 if down else 0) else "swp"
                    name = kind + str(step) + lane
                table[core, away, owner] = NAMES.index(name)
    return table


def pick(slot, low, high, use):
    if high - low == 1:
        use(low)
        return
    middle = (low + high) // 2

    @pl.when(slot < middle)
    def _():
        pick(slot, low, middle, use)

    @pl.when(slot >= middle)
    def _():
        pick(slot, middle, high, use)


def join_kernel(*refs):
    parts, joined, sems = refs[:4], refs[4], refs[5]
    copies = [
        pltpu.make_async_copy(part, joined.at[:, n * WIDTH : (n + 1) * WIDTH], sems.at[n])
        for n, part in enumerate(parts)
    ]
    for copy in copies:
        copy.start()
    for copy in copies:
        copy.wait()


def join(parts):
    return pl.pallas_call(
        join_kernel,
        out_shape=jax.ShapeDtypeStruct((BLK, 4 * WIDTH), jnp.bfloat16),
        in_specs=[pl.BlockSpec(memory_space=pltpu.HBM)] * 4,
        out_specs=pl.BlockSpec(memory_space=pltpu.VMEM),
        scratch_shapes=[pltpu.SemaphoreType.DMA((4,))],
        compiler_params=pltpu.CompilerParams(vmem_limit_bytes=60 << 20),
        cost_estimate=pl.CostEstimate(flops=0, bytes_accessed=1 << 20, transcendentals=0),
    )(*parts)


OVER_ROWS = (((1,), (1,)), ((), ()))
OVER_KEYS = (((1,), (0,)), ((), ()))


def head_columns(h):
    return slice(h * DH, (h + 1) * DH)


def group_queries(q_ref, g):
    return jnp.concatenate([q_ref[:, head_columns(h)] for h in range(g * GROUP, (g + 1) * GROUP)], axis=0)


def near_kernel(
    me_ref, table_ref, lists_ref, q_ref, own_ref, oth_ref, got_ref, total_ref, sum_ref, top_ref, slot_ref, half_ref, new, old, sems
):
    me = me_ref[0]
    core = lax.rem(me, 2)
    column = pl.multiple_of(jnp.where(me == 0, 0, 2 * WIDTH), 2 * WIDTH)
    own_copy = pltpu.make_async_copy(own_ref.at[:, 2 * WIDTH :], new, sems.at[0])
    own_copy.start()

    def old_copy(source):
        return pltpu.make_async_copy(source.at[:, pl.ds(column, 2 * WIDTH)], old, sems.at[1])

    @pl.when(core == 1)
    def _():
        old_copy(oth_ref).start()

    @pl.when(core == 0)
    def _():
        old_copy(got_ref).start()

    def locate(h, carry):
        chosen = lists_ref[4 * h] + lists_ref[4 * h + 1] + lists_ref[4 * h + 2] + lists_ref[4 * h + 3]
        chosen = jnp.clip(chosen - (2 * (SEQ + me) - 1), 0, 2 * SEQ - 1)
        owner = lax.rem(chosen, SEQ)
        away = lax.rem(owner // 2 - me // 2 + CHIPS, CHIPS)
        slot_ref[h] = table_ref[core * 2 * CHIPS + away * 2 + lax.rem(owner, 2)]
        half_ref[h] = chosen // SEQ
        return carry

    lax.fori_loop(0, HEADS, locate, 0)
    own_copy.wait()
    old_copy(oth_ref).wait()

    seen = lax.broadcasted_iota(jnp.int32, (BLK, BLK), 1) <= lax.broadcasted_iota(jnp.int32, (BLK, BLK), 0)
    ones = jnp.ones((2 * BLK, DH), jnp.bfloat16)
    for h in range(HEADS):
        g, cols = h // GROUP, head_columns(h)
        keys = jnp.concatenate([old[:, head_columns(g)], new[:, head_columns(g)]], axis=0)
        values = jnp.concatenate([old[:, head_columns(KVH + g)], new[:, head_columns(KVH + g)]], axis=0)
        scores = lax.dot_general(q_ref[:, cols], keys, OVER_ROWS, preferred_element_type=jnp.float32)
        scores = jnp.concatenate([scores[:, :BLK], jnp.where(seen, scores[:, BLK:], -jnp.inf)], axis=1)
        top = jnp.max(scores, axis=1, keepdims=True)
        powers = jnp.exp2((scores - top) * SCALE).astype(jnp.bfloat16)
        mixed = lax.dot_general(
            powers, jnp.concatenate([values, ones], axis=1), OVER_KEYS, preferred_element_type=jnp.float32
        )
        total_ref[:, cols] = mixed[:, :DH]
        sum_ref[:, cols] = mixed[:, DH:]
        top_ref[:, cols] = jnp.broadcast_to(top, (BLK, DH))


def near(me, table, lists, queries, own, oth, got):
    smem, vmem = pl.BlockSpec(memory_space=pltpu.SMEM), pl.BlockSpec(memory_space=pltpu.VMEM)
    anywhere = pl.BlockSpec(memory_space=pl.ANY)
    return pl.pallas_call(
        near_kernel,
        out_shape=[
            jax.ShapeDtypeStruct((BLK, HEADS * DH), jnp.float32),
            jax.ShapeDtypeStruct((BLK, HEADS * DH), jnp.float32),
            jax.ShapeDtypeStruct((BLK, HEADS * DH), jnp.float32),
            jax.ShapeDtypeStruct((HEADS,), jnp.int32),
            jax.ShapeDtypeStruct((HEADS,), jnp.int32),
        ],
        in_specs=[smem] * 3 + [vmem] + [anywhere] * 3,
        out_specs=[vmem, vmem, vmem, smem, smem],
        scratch_shapes=[
            pltpu.VMEM((BLK, 2 * WIDTH), jnp.bfloat16),
            pltpu.VMEM((BLK, 2 * WIDTH), jnp.bfloat16),
            pltpu.SemaphoreType.DMA((2,)),
        ],
        compiler_params=pltpu.CompilerParams(vmem_limit_bytes=20 << 20),
        cost_estimate=pl.CostEstimate(flops=1 << 29, bytes_accessed=4 << 20, transcendentals=1 << 20),
    )(me, table, lists, queries, own, oth, got)


def far_kernel(me_ref, table_ref, slot_ref, half_ref, q_ref, total_ref, sum_ref, top_ref, *refs):
    held = refs[: len(NAMES)]
    o_ref, first, k_pick, v_pick = refs[len(NAMES) :]
    me = me_ref[0]
    slot = table_ref[lax.rem(me, 2) * 2 * CHIPS + lax.rem(CHIPS - me // 2, CHIPS) * 2]

    def take_first(b):
        first[...] = held[b][:, : 2 * WIDTH]

    pick(slot, 0, len(NAMES), take_first)

    def take_head(h, carry):
        column = pl.multiple_of(half_ref[h] * 2 * WIDTH + (h // GROUP) * DH, DH)

        def take(b):
            k_pick[h] = held[b][:, pl.ds(column, DH)]
            v_pick[h] = held[b][:, pl.ds(column + WIDTH, DH)]

        pick(slot_ref[h], 0, len(NAMES), take)
        return carry

    lax.fori_loop(0, HEADS, take_head, 0, unroll=4)
    ones = jnp.ones((2 * BLK, DH), jnp.bfloat16)
    for h in range(HEADS):
        g, cols = h // GROUP, head_columns(h)
        keys = jnp.concatenate([first[:, head_columns(g)], k_pick[h]], axis=0)
        values = jnp.concatenate([first[:, head_columns(KVH + g)], v_pick[h]], axis=0)
        scores = lax.dot_general(q_ref[:, cols], keys, OVER_ROWS, preferred_element_type=jnp.float32)
        top = jnp.maximum(jnp.max(scores, axis=1, keepdims=True), top_ref[:, cols])
        powers = jnp.exp2((scores - jnp.concatenate([top, top], axis=1)) * SCALE).astype(jnp.bfloat16)
        factor = jnp.exp2((top_ref[:, cols] - top) * SCALE)
        mixed = lax.dot_general(
            powers, jnp.concatenate([values, ones], axis=1), OVER_KEYS, preferred_element_type=jnp.float32
        )
        total = mixed[:, :DH] + factor * total_ref[:, cols]
        weight = mixed[:, DH:] + factor * sum_ref[:, cols]
        o_ref[:, cols] = (total / weight).astype(jnp.bfloat16)


def tie_kernel(through_in, after, through_out):
    pass


def tie(through, after):
    return pl.pallas_call(
        tie_kernel,
        out_shape=jax.ShapeDtypeStruct(through.shape, through.dtype),
        in_specs=[pl.BlockSpec(memory_space=pl.ANY)] * 2,
        out_specs=pl.BlockSpec(memory_space=pl.ANY),
        input_output_aliases={0: 0},
        compiler_params=pltpu.CompilerParams(vmem_limit_bytes=1 << 20),
    )(through, after)


def far(me, table, slots, halves, queries, near_parts, held):
    smem, vmem = pl.BlockSpec(memory_space=pltpu.SMEM), pl.BlockSpec(memory_space=pltpu.VMEM)
    return pl.pallas_call(
        far_kernel,
        out_shape=jax.ShapeDtypeStruct((BLK, HEADS * DH), jnp.bfloat16),
        in_specs=[smem] * 4 + [vmem] * (4 + len(NAMES)),
        out_specs=vmem,
        scratch_shapes=[
            pltpu.VMEM((BLK, 2 * WIDTH), jnp.bfloat16),
            pltpu.VMEM((HEADS, BLK, DH), jnp.bfloat16),
            pltpu.VMEM((HEADS, BLK, DH), jnp.bfloat16),
        ],
        compiler_params=pltpu.CompilerParams(vmem_limit_bytes=24 << 20),
        cost_estimate=pl.CostEstimate(flops=1 << 29, bytes_accessed=6 << 20, transcendentals=1 << 20),
    )(me, table, slots, halves, queries, *near_parts, *held)


def shards(queries, span_keys, span_values, cache_keys, cache_values, block_lists):
    me = lax.axis_index("seq").astype(jnp.int32).reshape(1)
    table = jnp.asarray(slot_table().reshape(-1))
    own = join([cache_keys, cache_values, span_keys, span_values])
    held = {"own": own}
    last = {}
    for step in (1, 2, 3, 4):
        for lane in ("A", "B"):
            if (step, lane) == (4, "B"):
                continue
            if step == 1:
                last[lane] = lax.ppermute(own, "seq", RING if lane == "A" else CROSS)
            else:
                if (step, lane) == (3, "A"):
                    last[lane] = tie(last[lane], slots)
                    held["got2A"] = last[lane]
                    held["swp2A"] = lax.ppermute(last[lane], "seq", SWAP)
                last[lane] = lax.ppermute(last[lane], "seq", RING)
            held["got" + str(step) + lane] = last[lane]
            if (step, lane) == (1, "B"):
                held["oth"] = lax.ppermute(own, "seq", SWAP)
                total, sums, tops, slots, halves = near(
                    me, table, block_lists.reshape(-1), queries, own, held["oth"], held["got1B"]
                )
            if (step, lane) != (2, "A"):
                held["swp" + str(step) + lane] = lax.ppermute(last[lane], "seq", SWAP)
    return far(me, table, slots, halves, queries, (total, sums, tops), [held[name] for name in NAMES])


def solution(mesh):
    rows = P(("req", "seq"), None)
    return jax.shard_map(
        shards,
        mesh=mesh,
        in_specs=(rows,) * 5 + (P(("req", "seq"), None, None),),
        out_specs=rows,
        check_vma=False,
    )
```

```python
import math

import jax
import jax.numpy as jnp
import numpy as np
from jax import lax
from jax.experimental import pallas as pl
from jax.experimental.pallas import tpu as pltpu
from jax.sharding import PartitionSpec as P

HEADS = 32
KVH = 4
GROUP = HEADS // KVH
DH = 128
BLK = 128
WIDTH = KVH * DH
SEQ = 16
CHIPS = SEQ // 2
SCALE = math.log2(math.e) / math.sqrt(DH)

RING = [(2 * z, 2 * ((z + 1) % CHIPS)) for z in range(CHIPS)] + [
    (2 * z + 1, 2 * ((z - 1) % CHIPS) + 1) for z in range(CHIPS)
]
CROSS = [(2 * z + 1, 2 * ((z + 1) % CHIPS)) for z in range(CHIPS)] + [
    (2 * z, 2 * ((z - 1) % CHIPS) + 1) for z in range(CHIPS)
]
SWAP = [(i, i ^ 1) for i in range(SEQ)]

NAMES = ["own", "oth"] + [
    kind + str(step) + lane
    for step in (1, 2, 3, 4)
    for lane in ("A", "B")
    for kind in ("got", "swp")
    if (step, lane) != (4, "B")
]


def slot_table():
    table = np.zeros((2, CHIPS, 2), np.int32)
    for core in range(2):
        for away in range(CHIPS):
            for owner in range(2):
                if away == 0:
                    name = "own" if owner == core else "oth"
                else:
                    down = away < 4 or (away == 4 and owner == 1)
                    step = away if down else CHIPS - away
                    lane = "A" if owner == (1 if down else 0) else "B"
                    kind = "got" if core == (1 if down else 0) else "swp"
                    name = kind + str(step) + lane
                table[core, away, owner] = NAMES.index(name)
    return table


def pick(slot, low, high, use):
    if high - low == 1:
        use(low)
        return
    middle = (low + high) // 2

    @pl.when(slot < middle)
    def _():
        pick(slot, low, middle, use)

    @pl.when(slot >= middle)
    def _():
        pick(slot, middle, high, use)


def join_kernel(*refs):
    parts, joined, sems = refs[:4], refs[4], refs[5]
    copies = [
        pltpu.make_async_copy(part, joined.at[:, n * WIDTH : (n + 1) * WIDTH], sems.at[n])
        for n, part in enumerate(parts)
    ]
    for copy in copies:
        copy.start()
    for copy in copies:
        copy.wait()


def join(parts):
    return pl.pallas_call(
        join_kernel,
        out_shape=jax.ShapeDtypeStruct((BLK, 4 * WIDTH), jnp.bfloat16),
        in_specs=[pl.BlockSpec(memory_space=pltpu.HBM)] * 4,
        out_specs=pl.BlockSpec(memory_space=pltpu.VMEM),
        scratch_shapes=[pltpu.SemaphoreType.DMA((4,))],
        compiler_params=pltpu.CompilerParams(vmem_limit_bytes=60 << 20),
        cost_estimate=pl.CostEstimate(flops=0, bytes_accessed=1 << 20, transcendentals=0),
    )(*parts)


OVER_ROWS = (((1,), (1,)), ((), ()))
OVER_KEYS = (((1,), (0,)), ((), ()))


def head_columns(h):
    return slice(h * DH, (h + 1) * DH)


def group_queries(q_ref, g):
    return jnp.concatenate([q_ref[:, head_columns(h)] for h in range(g * GROUP, (g + 1) * GROUP)], axis=0)


def near_kernel(
    me_ref, table_ref, lists_ref, q_ref, own_ref, oth_ref, got_ref, total_ref, sum_ref, top_ref, slot_ref, half_ref, new, old, sems
):
    me = me_ref[0]
    core = lax.rem(me, 2)
    column = pl.multiple_of(jnp.where(me == 0, 0, 2 * WIDTH), 2 * WIDTH)
    own_copy = pltpu.make_async_copy(own_ref.at[:, 2 * WIDTH :], new, sems.at[0])
    own_copy.start()

    def old_copy(source):
        return pltpu.make_async_copy(source.at[:, pl.ds(column, 2 * WIDTH)], old, sems.at[1])

    @pl.when(core == 1)
    def _():
        old_copy(oth_ref).start()

    @pl.when(core == 0)
    def _():
        old_copy(got_ref).start()

    def locate(h, carry):
        chosen = lists_ref[4 * h] + lists_ref[4 * h + 1] + lists_ref[4 * h + 2] + lists_ref[4 * h + 3]
        chosen = jnp.clip(chosen - (2 * (SEQ + me) - 1), 0, 2 * SEQ - 1)
        owner = lax.rem(chosen, SEQ)
        away = lax.rem(owner // 2 - me // 2 + CHIPS, CHIPS)
        slot_ref[h] = table_ref[core * 2 * CHIPS + away * 2 + lax.rem(owner, 2)]
        half_ref[h] = chosen // SEQ
        return carry

    lax.fori_loop(0, HEADS, locate, 0)
    own_copy.wait()
    old_copy(oth_ref).wait()

    seen = lax.broadcasted_iota(jnp.int32, (BLK, BLK), 1) <= lax.broadcasted_iota(jnp.int32, (BLK, BLK), 0)
    ones = jnp.ones((2 * BLK, DH), jnp.bfloat16)
    for h in range(HEADS):
        g, cols = h // GROUP, head_columns(h)
        keys = jnp.concatenate([old[:, head_columns(g)], new[:, head_columns(g)]], axis=0)
        values = jnp.concatenate([old[:, head_columns(KVH + g)], new[:, head_columns(KVH + g)]], axis=0)
        scores = lax.dot_general(q_ref[:, cols], keys, OVER_ROWS, preferred_element_type=jnp.float32)
        scores = jnp.concatenate([scores[:, :BLK], jnp.where(seen, scores[:, BLK:], -jnp.inf)], axis=1)
        top = jnp.max(scores, axis=1, keepdims=True)
        powers = jnp.exp2((scores - top) * SCALE).astype(jnp.bfloat16)
        mixed = lax.dot_general(
            powers, jnp.concatenate([values, ones], axis=1), OVER_KEYS, preferred_element_type=jnp.float32
        )
        total_ref[:, cols] = mixed[:, :DH]
        sum_ref[:, cols] = mixed[:, DH:]
        top_ref[:, cols] = jnp.broadcast_to(top, (BLK, DH))


def near(me, table, lists, queries, own, oth, got):
    smem, vmem = pl.BlockSpec(memory_space=pltpu.SMEM), pl.BlockSpec(memory_space=pltpu.VMEM)
    anywhere = pl.BlockSpec(memory_space=pl.ANY)
    return pl.pallas_call(
        near_kernel,
        out_shape=[
            jax.ShapeDtypeStruct((BLK, HEADS * DH), jnp.float32),
            jax.ShapeDtypeStruct((BLK, HEADS * DH), jnp.float32),
            jax.ShapeDtypeStruct((BLK, HEADS * DH), jnp.float32),
            jax.ShapeDtypeStruct((HEADS,), jnp.int32),
            jax.ShapeDtypeStruct((HEADS,), jnp.int32),
        ],
        in_specs=[smem] * 3 + [vmem] + [anywhere] * 3,
        out_specs=[vmem, vmem, vmem, smem, smem],
        scratch_shapes=[
            pltpu.VMEM((BLK, 2 * WIDTH), jnp.bfloat16),
            pltpu.VMEM((BLK, 2 * WIDTH), jnp.bfloat16),
            pltpu.SemaphoreType.DMA((2,)),
        ],
        compiler_params=pltpu.CompilerParams(vmem_limit_bytes=20 << 20),
        cost_estimate=pl.CostEstimate(flops=1 << 29, bytes_accessed=4 << 20, transcendentals=1 << 20),
    )(me, table, lists, queries, own, oth, got)


def far_kernel(me_ref, table_ref, slot_ref, half_ref, q_ref, total_ref, sum_ref, top_ref, *refs):
    held = refs[: len(NAMES)]
    o_ref, first, k_pick, v_pick = refs[len(NAMES) :]
    me = me_ref[0]
    slot = table_ref[lax.rem(me, 2) * 2 * CHIPS + lax.rem(CHIPS - me // 2, CHIPS) * 2]

    def take_first(b):
        first[...] = held[b][:, : 2 * WIDTH]

    pick(slot, 0, len(NAMES), take_first)

    def take_head(h, carry):
        column = pl.multiple_of(half_ref[h] * 2 * WIDTH + (h // GROUP) * DH, DH)

        def take(b):
            k_pick[h] = held[b][:, pl.ds(column, DH)]
            v_pick[h] = held[b][:, pl.ds(column + WIDTH, DH)]

        pick(slot_ref[h], 0, len(NAMES), take)
        return carry

    lax.fori_loop(0, HEADS, take_head, 0, unroll=32)
    ones = jnp.ones((2 * BLK, DH), jnp.bfloat16)
    for h in range(HEADS):
        g, cols = h // GROUP, head_columns(h)
        keys = jnp.concatenate([first[:, head_columns(g)], k_pick[h]], axis=0)
        values = jnp.concatenate([first[:, head_columns(KVH + g)], v_pick[h]], axis=0)
        scores = lax.dot_general(q_ref[:, cols], keys, OVER_ROWS, preferred_element_type=jnp.float32)
        top = jnp.maximum(jnp.max(scores, axis=1, keepdims=True), top_ref[:, cols])
        powers = jnp.exp2((scores - jnp.concatenate([top, top], axis=1)) * SCALE).astype(jnp.bfloat16)
        factor = jnp.exp2((top_ref[:, cols] - top) * SCALE)
        mixed = lax.dot_general(
            powers, jnp.concatenate([values, ones], axis=1), OVER_KEYS, preferred_element_type=jnp.float32
        )
        total = mixed[:, :DH] + factor * total_ref[:, cols]
        weight = mixed[:, DH:] + factor * sum_ref[:, cols]
        o_ref[:, cols] = (total / weight).astype(jnp.bfloat16)


def tie_kernel(through_in, after, through_out):
    pass


def tie(through, after):
    return pl.pallas_call(
        tie_kernel,
        out_shape=jax.ShapeDtypeStruct(through.shape, through.dtype),
        in_specs=[pl.BlockSpec(memory_space=pl.ANY)] * 2,
        out_specs=pl.BlockSpec(memory_space=pl.ANY),
        input_output_aliases={0: 0},
        compiler_params=pltpu.CompilerParams(vmem_limit_bytes=1 << 20),
    )(through, after)


def far(me, table, slots, halves, queries, near_parts, held):
    smem, vmem = pl.BlockSpec(memory_space=pltpu.SMEM), pl.BlockSpec(memory_space=pltpu.VMEM)
    return pl.pallas_call(
        far_kernel,
        out_shape=jax.ShapeDtypeStruct((BLK, HEADS * DH), jnp.bfloat16),
        in_specs=[smem] * 4 + [vmem] * (4 + len(NAMES)),
        out_specs=vmem,
        scratch_shapes=[
            pltpu.VMEM((BLK, 2 * WIDTH), jnp.bfloat16),
            pltpu.VMEM((HEADS, BLK, DH), jnp.bfloat16),
            pltpu.VMEM((HEADS, BLK, DH), jnp.bfloat16),
        ],
        compiler_params=pltpu.CompilerParams(vmem_limit_bytes=24 << 20),
        cost_estimate=pl.CostEstimate(flops=1 << 29, bytes_accessed=6 << 20, transcendentals=1 << 20),
    )(me, table, slots, halves, queries, *near_parts, *held)


def shards(queries, span_keys, span_values, cache_keys, cache_values, block_lists):
    me = lax.axis_index("seq").astype(jnp.int32).reshape(1)
    table = jnp.asarray(slot_table().reshape(-1))
    own = join([cache_keys, cache_values, span_keys, span_values])
    held = {"own": own}
    last = {}
    for step in (1, 2, 3, 4):
        for lane in ("A", "B"):
            if (step, lane) == (4, "B"):
                continue
            if step == 1:
                last[lane] = lax.ppermute(own, "seq", RING if lane == "A" else CROSS)
            else:
                if (step, lane) == (3, "A"):
                    last[lane] = tie(last[lane], slots)
                    held["got2A"] = last[lane]
                    held["swp2A"] = lax.ppermute(last[lane], "seq", SWAP)
                last[lane] = lax.ppermute(last[lane], "seq", RING)
            held["got" + str(step) + lane] = last[lane]
            if (step, lane) == (1, "B"):
                held["oth"] = lax.ppermute(own, "seq", SWAP)
                total, sums, tops, slots, halves = near(
                    me, table, block_lists.reshape(-1), queries, own, held["oth"], held["got1B"]
                )
            if (step, lane) != (2, "A"):
                held["swp" + str(step) + lane] = lax.ppermute(last[lane], "seq", SWAP)
    return far(me, table, slots, halves, queries, (total, sums, tops), [held[name] for name in NAMES])


def solution(mesh):
    rows = P(("req", "seq"), None)
    return jax.shard_map(
        shards,
        mesh=mesh,
        in_specs=(rows,) * 5 + (P(("req", "seq"), None, None),),
        out_specs=rows,
        check_vma=False,
    )
```

```python
import math

import jax
import jax.numpy as jnp
import numpy as np
from jax import lax
from jax.experimental import pallas as pl
from jax.experimental.pallas import tpu as pltpu
from jax.sharding import PartitionSpec as P

HEADS = 32
KVH = 4
GROUP = HEADS // KVH
DH = 128
BLK = 128
WIDTH = KVH * DH
SEQ = 16
CHIPS = SEQ // 2
SCALE = math.log2(math.e) / math.sqrt(DH)

RING = [(2 * z, 2 * ((z + 1) % CHIPS)) for z in range(CHIPS)] + [
    (2 * z + 1, 2 * ((z - 1) % CHIPS) + 1) for z in range(CHIPS)
]
CROSS = [(2 * z + 1, 2 * ((z + 1) % CHIPS)) for z in range(CHIPS)] + [
    (2 * z, 2 * ((z - 1) % CHIPS) + 1) for z in range(CHIPS)
]
SWAP = [(i, i ^ 1) for i in range(SEQ)]

RING_LATE = [(source, target) for source, target in RING if source < target and source >= SEQ // 2 - 2 and source % 2 == 0]
SHARE_LATE = [(target, target + 1) for source, target in RING_LATE]

NAMES = ["own", "oth"] + [kind + step for step in ("1", "2", "3", "4C", "4S") for kind in ("g", "s")]
COLUMNS = 40


def place_table():
    table = np.zeros((2, 2, 2, CHIPS, 2), np.int32)
    for part, core, away, owner in np.ndindex(*table.shape[1:]):
        column = 2 * WIDTH * part
        if away == 0:
            name = "own" if owner == core else "oth"
        else:
            down = away < 4 or (away == 4 and owner == 1)
            step = away if down else CHIPS - away
            lane_b = owner != (1 if down else 0)
            name = ("g" if core == (1 if down else 0) else "s") + str(step)
            if step < 4:
                column += 4 * WIDTH * lane_b
            else:
                name, column = ("gs"[core] + "4S", 2 * WIDTH * owner) if part else (name + "C", 0)
        table[:, part, core, away, owner] = NAMES.index(name), column
    return table.reshape(-1)


def pick(slot, low, high, use):
    if high - low == 1:
        use(low)
        return
    middle = (low + high) // 2

    @pl.when(slot < middle)
    def _():
        pick(slot, low, middle, use)

    @pl.when(slot >= middle)
    def _():
        pick(slot, middle, high, use)


def join_kernel(*refs):
    parts, joined, sems = refs[:4], refs[4], refs[5]
    copies = [
        pltpu.make_async_copy(part, joined.at[:, n * WIDTH : (n + 1) * WIDTH], sems.at[n])
        for n, part in enumerate(parts)
    ]
    for copy in copies:
        copy.start()
    for copy in copies:
        copy.wait()


def join(parts):
    return pl.pallas_call(
        join_kernel,
        out_shape=jax.ShapeDtypeStruct((BLK, 4 * WIDTH), jnp.bfloat16),
        in_specs=[pl.BlockSpec(memory_space=pltpu.HBM)] * 4,
        out_specs=pl.BlockSpec(memory_space=pltpu.VMEM),
        scratch_shapes=[pltpu.SemaphoreType.DMA((4,))],
        compiler_params=pltpu.CompilerParams(vmem_limit_bytes=60 << 20),
        cost_estimate=pl.CostEstimate(flops=0, bytes_accessed=1 << 20, transcendentals=0),
    )(*parts)


OVER_ROWS = (((1,), (1,)), ((), ()))
OVER_KEYS = (((1,), (0,)), ((), ()))


def head_columns(h):
    return slice(h * DH, (h + 1) * DH)


def group_queries(q_ref, g):
    return jnp.concatenate([q_ref[:, head_columns(h)] for h in range(g * GROUP, (g + 1) * GROUP)], axis=0)


def near_kernel(
    me_ref, table_ref, lists_ref, q_ref, own_ref, oth_ref, got_ref, total_ref, sum_ref, top_ref, place_ref, new, old, sems
):
    me = me_ref[0]
    core = lax.rem(me, 2)
    column = pl.multiple_of(jnp.where(me == 0, 0, 2 * WIDTH), 2 * WIDTH)
    own_copy = pltpu.make_async_copy(own_ref.at[:, 2 * WIDTH :], new, sems.at[0])
    own_copy.start()

    def old_copy(source):
        return pltpu.make_async_copy(source.at[:, pl.ds(column, 2 * WIDTH)], old, sems.at[1])

    @pl.when(core == 1)
    def _():
        old_copy(oth_ref).start()

    @pl.when(core == 0)
    def _():
        old_copy(got_ref).start()

    def place(n, block, column):
        owner = lax.rem(block, SEQ)
        away = lax.rem(owner // 2 - me // 2 + CHIPS, CHIPS)
        entry = block // SEQ * 4 * CHIPS + core * 2 * CHIPS + away * 2 + lax.rem(owner, 2)
        place_ref[n] = table_ref[entry]
        place_ref[COLUMNS + n] = table_ref[8 * CHIPS + entry] + column

    def locate(h, carry):
        chosen = lists_ref[4 * h] + lists_ref[4 * h + 1] + lists_ref[4 * h + 2] + lists_ref[4 * h + 3]
        place(h, jnp.clip(chosen - (2 * (SEQ + me) - 1), 0, 2 * SEQ - 1), h // GROUP * DH)
        return carry

    lax.fori_loop(0, HEADS, locate, 0)
    place(HEADS, jnp.int32(0), 0)
    own_copy.wait()
    old_copy(oth_ref).wait()

    seen = lax.broadcasted_iota(jnp.int32, (BLK, BLK), 1) <= lax.broadcasted_iota(jnp.int32, (BLK, BLK), 0)
    ones = jnp.ones((2 * BLK, DH), jnp.bfloat16)
    for h in range(HEADS):
        g, cols = h // GROUP, head_columns(h)
        keys = jnp.concatenate([old[:, head_columns(g)], new[:, head_columns(g)]], axis=0)
        values = jnp.concatenate([old[:, head_columns(KVH + g)], new[:, head_columns(KVH + g)]], axis=0)
        scores = lax.dot_general(q_ref[:, cols], keys, OVER_ROWS, preferred_element_type=jnp.float32)
        scores = jnp.concatenate([scores[:, :BLK], jnp.where(seen, scores[:, BLK:], -jnp.inf)], axis=1)
        top = jnp.max(scores, axis=1, keepdims=True)
        powers = jnp.exp2((scores - top) * SCALE).astype(jnp.bfloat16)
        mixed = lax.dot_general(
            powers, jnp.concatenate([values, ones], axis=1), OVER_KEYS, preferred_element_type=jnp.float32
        )
        total_ref[:, cols] = mixed[:, :DH]
        sum_ref[:, cols] = mixed[:, DH:]
        top_ref[:, cols] = jnp.broadcast_to(top, (BLK, DH))


def near(me, table, lists, queries, own, oth, got):
    smem, vmem = pl.BlockSpec(memory_space=pltpu.SMEM), pl.BlockSpec(memory_space=pltpu.VMEM)
    anywhere = pl.BlockSpec(memory_space=pl.ANY)
    return pl.pallas_call(
        near_kernel,
        out_shape=[
            jax.ShapeDtypeStruct((BLK, HEADS * DH), jnp.float32),
            jax.ShapeDtypeStruct((BLK, HEADS * DH), jnp.float32),
            jax.ShapeDtypeStruct((BLK, HEADS * DH), jnp.float32),
            jax.ShapeDtypeStruct((2 * COLUMNS,), jnp.int32),
        ],
        in_specs=[smem] * 3 + [vmem] + [anywhere] * 3,
        out_specs=[vmem, vmem, vmem, smem],
        scratch_shapes=[
            pltpu.VMEM((BLK, 2 * WIDTH), jnp.bfloat16),
            pltpu.VMEM((BLK, 2 * WIDTH), jnp.bfloat16),
            pltpu.SemaphoreType.DMA((2,)),
        ],
        compiler_params=pltpu.CompilerParams(vmem_limit_bytes=20 << 20),
        cost_estimate=pl.CostEstimate(flops=1 << 29, bytes_accessed=4 << 20, transcendentals=1 << 20),
    )(me, table, lists, queries, own, oth, got)


def far_kernel(place_ref, q_ref, total_ref, sum_ref, top_ref, *refs):
    held = refs[: len(NAMES)]
    o_ref, first, k_pick, v_pick = refs[len(NAMES) :]
    first_column = pl.multiple_of(place_ref[COLUMNS + HEADS], DH)

    def take_first(b):
        first[...] = held[b][:, pl.ds(first_column, 2 * WIDTH)]

    pick(place_ref[HEADS], 0, len(NAMES), take_first)

    def take_head(h, carry):
        column = pl.multiple_of(place_ref[COLUMNS + h], DH)

        def take(b):
            k_pick[h] = held[b][:, pl.ds(column, DH)]
            v_pick[h] = held[b][:, pl.ds(column + WIDTH, DH)]

        pick(place_ref[h], 0, len(NAMES), take)
        return carry

    lax.fori_loop(0, HEADS, take_head, 0, unroll=32)
    ones = jnp.ones((2 * BLK, DH), jnp.bfloat16)
    for h in range(HEADS):
        g, cols = h // GROUP, head_columns(h)
        keys = jnp.concatenate([first[:, head_columns(g)], k_pick[h]], axis=0)
        values = jnp.concatenate([first[:, head_columns(KVH + g)], v_pick[h]], axis=0)
        scores = lax.dot_general(q_ref[:, cols], keys, OVER_ROWS, preferred_element_type=jnp.float32)
        top = jnp.maximum(jnp.max(scores, axis=1, keepdims=True), top_ref[:, cols])
        powers = jnp.exp2((scores - jnp.concatenate([top, top], axis=1)) * SCALE).astype(jnp.bfloat16)
        factor = jnp.exp2((top_ref[:, cols] - top) * SCALE)
        mixed = lax.dot_general(
            powers, jnp.concatenate([values, ones], axis=1), OVER_KEYS, preferred_element_type=jnp.float32
        )
        total = mixed[:, :DH] + factor * total_ref[:, cols]
        weight = mixed[:, DH:] + factor * sum_ref[:, cols]
        o_ref[:, cols] = (total / weight).astype(jnp.bfloat16)


def tie_kernel(through_in, after, through_out):
    pass


def tie(through, after, flops=0):
    return pl.pallas_call(
        tie_kernel,
        out_shape=jax.ShapeDtypeStruct(through.shape, through.dtype),
        in_specs=[pl.BlockSpec(memory_space=pl.ANY)] * 2,
        out_specs=pl.BlockSpec(memory_space=pl.ANY),
        input_output_aliases={0: 0},
        compiler_params=pltpu.CompilerParams(vmem_limit_bytes=1 << 20),
        cost_estimate=pl.CostEstimate(flops=flops, bytes_accessed=0, transcendentals=0),
    )(through, after)


def far(places, queries, near_parts, held):
    smem, vmem = pl.BlockSpec(memory_space=pltpu.SMEM), pl.BlockSpec(memory_space=pltpu.VMEM)
    return pl.pallas_call(
        far_kernel,
        out_shape=jax.ShapeDtypeStruct((BLK, HEADS * DH), jnp.bfloat16),
        in_specs=[smem] + [vmem] * (4 + len(NAMES)),
        out_specs=vmem,
        scratch_shapes=[
            pltpu.VMEM((BLK, 2 * WIDTH), jnp.bfloat16),
            pltpu.VMEM((HEADS, BLK, DH), jnp.bfloat16),
            pltpu.VMEM((HEADS, BLK, DH), jnp.bfloat16),
        ],
        compiler_params=pltpu.CompilerParams(vmem_limit_bytes=24 << 20),
        cost_estimate=pl.CostEstimate(flops=1 << 29, bytes_accessed=6 << 20, transcendentals=1 << 20),
    )(places, queries, *near_parts, *held)


def shards(queries, span_keys, span_values, cache_keys, cache_values, block_lists):
    me = lax.axis_index("seq").astype(jnp.int32).reshape(1)
    table = jnp.asarray(place_table())

    def send(x, pairs):
        return lax.ppermute(x, "seq", pairs)

    held = {"own": join([cache_keys, cache_values, span_keys, span_values])}
    lane_a, lane_b = send(held["own"], RING), send(held["own"], CROSS)
    held["oth"] = send(held["own"], SWAP)
    *near_parts, places = near(me, table, block_lists.reshape(-1), queries, held["own"], held["oth"], lane_b)
    held["g1"] = jnp.concatenate([lane_a, lane_b], axis=1)
    lane_a, lane_b = tie(send(lane_a, RING), places), send(lane_b, RING)
    held["g2"] = jnp.concatenate([lane_a, lane_b], axis=1)
    lane_a, lane_b = send(lane_a, RING), send(lane_b, RING)
    held["g3"] = jnp.concatenate([lane_a, lane_b], axis=1)
    for name in ("1", "2", "3"):
        held["s" + name] = send(held["g" + name], SWAP)
    held["g4C"] = send(lane_a[:, : 2 * WIDTH], RING)
    held["s4C"] = send(tie(tie(held["g4C"], places, 1 << 34), held["s3"]), SWAP)
    held["g4S"] = send(jnp.concatenate([lane_a[:, 2 * WIDTH :], lane_b[:, 2 * WIDTH :]], axis=1), RING_LATE)
    held["s4S"] = send(held["g4S"], SHARE_LATE)
    held["s2"] = tie(held["s2"], places, 1 << 33)
    held["s4S"] = tie(held["s4S"], places, 1 << 33)
    return far(places, queries, near_parts, [held[name] for name in NAMES])


def solution(mesh):
    rows = P(("req", "seq"), None)
    return jax.shard_map(
        shards,
        mesh=mesh,
        in_specs=(rows,) * 5 + (P(("req", "seq"), None, None),),
        out_specs=rows,
        check_vma=False,
    )
```
